32 devices in a mesh: dp: 2 (over core), fsdp: 16 (over z, y, x).
Axes of the slice: x: 2, y: 2, z: 4, core: 2. Of those that a mesh axis runs over, the one named last changes fastest.
Arguments:
- tokens: bfloat16 [8192, 1088], P(('dp', 'fsdp')), may hold values from -6 to 6
- cotangent: bfloat16 [8192, 1088], P(('dp', 'fsdp')), may hold values from -6 to 6
- lengths: int32 [32, 4], P(('dp', 'fsdp')), may hold values from 0 to 256, as said below
- triple_weight: float32 [1088, 3264], P('fsdp'), may hold values from -0.21875 to 0.21875
- triple_momentum: float32 [1088, 3264], P('fsdp'), may hold values from -32 to 32
- triple_variance: float32 [1088, 3264], P('fsdp'), may hold values from 155.648 to 622.592
- merge_weight: float32 [1088, 1088], P('fsdp'), may hold values from -0.75 to 0.75
- merge_momentum: float32 [1088, 1088], P('fsdp'), may hold values from -6 to 6
- merge_variance: float32 [1088, 1088], P('fsdp'), may hold values from 17.2032 to 68.8128
- expand_weight: float32 [1088, 4352], P('fsdp'), may hold values from -0.1875 to 0.1875
- expand_momentum: float32 [1088, 4352], P('fsdp'), may hold values from -16 to 16
- expand_variance: float32 [1088, 4352], P('fsdp'), may hold values from 29.4912 to 116.3264
- shrink_weight: float32 [4352, 1088], P('fsdp'), may hold values from -0.09375 to 0.09375
- shrink_momentum: float32 [4352, 1088], P('fsdp'), may hold values from -32 to 32
- shrink_variance: float32 [4352, 1088], P('fsdp'), may hold values from 130.2528 to 521.0112
- vector_weight: float32 [12, 1088], P(None, 'fsdp'), may hold values from -1.2 to 1.4
- vector_momentum: float32 [12, 1088], P(None, 'fsdp'), may hold values from -32 to 32
- vector_variance: float32 [12, 1088], P(None, 'fsdp'), may hold values from 106.496 to 434.176
Outputs:
- layer_output: bfloat16 [8192, 1088], P(('dp', 'fsdp'))
- input_grad: bfloat16 [8192, 1088], P(('dp', 'fsdp'))
- triple_next: float32 [1088, 3264], P('fsdp')
- momentum_triple: float32 [1088, 3264], P('fsdp')
- variance_triple: float32 [1088, 3264], P('fsdp')
- merge_next: float32 [1088, 1088], P('fsdp')
- momentum_merge: float32 [1088, 1088], P('fsdp')
- variance_merge: float32 [1088, 1088], P('fsdp')
- expand_next: float32 [1088, 4352], P('fsdp')
- momentum_expand: float32 [1088, 4352], P('fsdp')
- variance_expand: float32 [1088, 4352], P('fsdp')
- shrink_next: float32 [4352, 1088], P('fsdp')
- momentum_shrink: float32 [4352, 1088], P('fsdp')
- variance_shrink: float32 [4352, 1088], P('fsdp')
- vector_next: float32 [12, 1088], P(None, 'fsdp')
- momentum_vector: float32 [12, 1088], P(None, 'fsdp')
- variance_vector: float32 [12, 1088], P(None, 'fsdp')
The draws below stay inside these ranges and needn't reach their ends.
Inputs may be any that keep to these rules, and one draw needn't show every extreme that they name: `lengths`: each row lists the sequences packed into one device's 256 slots from the start; the slots after their sum are padding. The first device holds one sequence of 256 tokens.
All inputs are finite; a program needn't handle non-finite values.
Results may differ from the reference program's by a relative error of at most 0.013.
The reference program's roundings to bfloat16 on the way count: a program that leaves them out, or rounds other values in their place, can miss the bound.
Values may be sent and summed in bfloat16 or wider, within the bound.
A program may use at most 192 MiB of HBM per device.

```python
import math
import jax
import jax.numpy as jnp
from jax import lax

D = 1088
HEADS = 17
HEAD_DIM = 64
FF = 4352
TOK_DEV = 256
SEQ_DEV = 4
STEP = 10
TOKENS = 8192
N_DP = 2
N_FSDP = 16


def draw_lengths(key, part):
    key = jax.random.fold_in(key, 7)
    first_key, second_key = jax.random.split(key)
    devices_all = N_DP * N_FSDP
    dropped = jax.random.randint(first_key, (N_DP,), 0, TOK_DEV // 2 + 1)
    live_replica = TOK_DEV - dropped
    live_device = jnp.repeat(live_replica, N_FSDP)
    raw_points = jax.random.randint(second_key, (devices_all, SEQ_DEV - 1), 0, TOK_DEV + 1)
    cut_points = jnp.sort(raw_points * (live_device[:, None] + 1) // (TOK_DEV + 1), axis=1)
    edge_points = jnp.concatenate([jnp.zeros((devices_all, 1), jnp.int32), cut_points.astype(jnp.int32), live_device[:, None].astype(jnp.int32)], axis=1)
    span_lengths = edge_points[:, 1:] - edge_points[:, :-1]
    first_device = jnp.where(jnp.arange(SEQ_DEV) == 0, TOK_DEV, 0).astype(jnp.int32)
    row_index = jnp.arange(devices_all)[:, None]
    return jnp.where(row_index == 0, first_device[None, :], span_lengths).astype(jnp.int32)


def draw_vector_weight(key, part):
    key = jax.random.fold_in(key, 11)
    gain_key, shift_key = jax.random.split(key)
    gains_all = jax.random.uniform(gain_key, (12, D), jnp.float32, 0.6, 1.4)
    shifts_all = 0.3 * jax.random.truncated_normal(shift_key, -4.0, 4.0, (12, D), jnp.float32)
    row_index = jnp.arange(12)[:, None]
    return jnp.where((row_index == 0) | (row_index == 5), gains_all, shifts_all)


def levels(key, shape, pieces, low, largest):
    factor_of = 1.0
    for dim, shards_of in pieces:
        heights = jax.random.uniform(jax.random.fold_in(jax.random.fold_in(key, 6), dim), (shards_of,), jnp.float32, low / len(pieces), largest / len(pieces))
        factor_of = factor_of * jnp.repeat(jnp.exp(heights), shape[dim] // shards_of).reshape((-1,) + (1,) * (len(shape) - 1 - dim))
    return factor_of


def normal_values(stream_key, dims, scale, reach, cuts=(), held_as=jnp.bfloat16):
    factor_of = levels(stream_key, dims, cuts, -0.22, 0.18) if cuts else 1.0
    values = jax.random.normal(stream_key, dims, jnp.float32) * scale * factor_of
    return jnp.minimum(jnp.maximum(values, -reach), reach).astype(held_as)


def setup_inputs(seed: int = 0) -> dict:
    key_list = jax.random.split(jax.random.key(seed), 19)
    tokens = normal_values(key_list[0], (TOKENS, D), 1.0, 6.0, ((0, 32),))
    cotangent = normal_values(key_list[1], (TOKENS, D), 1.0, 6.0, ((0, 32),))
    lengths = draw_lengths(jax.random.fold_in(key_list[18], 71), 0)
    triple_weight = normal_values(key_list[3], (D, 3 * D), (D * 2 // 3) ** -0.5, 0.21875, ((0, 16),), jnp.float32)
    triple_momentum = normal_values(key_list[4], (D, 3 * D), (0.067 * TOKENS ** 0.5), 32.0, ((0, 16),), jnp.float32)
    triple_variance = jnp.clip(jnp.exp(math.log(622.592) - 1.3862944 * jax.random.uniform(key_list[5], (D, 3 * D), jnp.float32) ** levels(key_list[5], (D, 3 * D), ((0, 16),), -0.2, 0.2)), 155.648, 622.592)
    merge_weight = normal_values(key_list[6], (D, D), (D // 16) ** -0.5, 0.75, ((0, 16),), jnp.float32)
    merge_momentum = normal_values(key_list[7], (D, D), (0.022 * TOKENS ** 0.5), 6.0, ((0, 16),), jnp.float32)
    merge_variance = jnp.clip(jnp.exp(math.log(68.8128) - 1.3862944 * jax.random.uniform(key_list[8], (D, D), jnp.float32) ** levels(key_list[8], (D, D), ((0, 16),), -0.2, 0.2)), 17.2032, 68.8128)
    expand_weight = normal_values(key_list[9], (D, FF), D ** -0.5, 0.1875, ((0, 16),), jnp.float32)
    expand_momentum = normal_values(key_list[10], (D, FF), (0.029 * TOKENS ** 0.5), 16.0, ((0, 16),), jnp.float32)
    expand_variance = jnp.clip(jnp.exp(math.log(116.3264) - 1.3723081 * jax.random.uniform(key_list[11], (D, FF), jnp.float32) ** levels(key_list[11], (D, FF), ((0, 16),), -0.2, 0.2)), 29.4912, 116.3264)
    shrink_weight = normal_values(key_list[12], (FF, D), FF ** -0.5, 0.09375, ((0, 16),), jnp.float32)
    shrink_momentum = normal_values(key_list[13], (FF, D), (0.061 * TOKENS ** 0.5), 32.0, ((0, 16),), jnp.float32)
    shrink_variance = jnp.clip(jnp.exp(math.log(521.0112) - 1.3862944 * jax.random.uniform(key_list[14], (FF, D), jnp.float32) ** levels(key_list[14], (FF, D), ((0, 16),), -0.2, 0.2)), 130.2528, 521.0112)
    vector_weight = draw_vector_weight(jax.random.fold_in(key_list[18], 71), 0)
    vector_momentum = normal_values(key_list[16], (12, D), (0.056 * TOKENS ** 0.5), 32.0, ((1, 16),), jnp.float32)
    vector_variance = jnp.clip(jnp.exp(math.log(434.176) - 1.40534252 * jax.random.uniform(key_list[17], (12, D), jnp.float32) ** levels(key_list[17], (12, D), ((1, 16),), -0.2, 0.2)), 106.496, 434.176)
    return dict(tokens=tokens, cotangent=cotangent, lengths=lengths, triple_weight=triple_weight, triple_momentum=triple_momentum, triple_variance=triple_variance, merge_weight=merge_weight, merge_momentum=merge_momentum, merge_variance=merge_variance, expand_weight=expand_weight, expand_momentum=expand_momentum, expand_variance=expand_variance, shrink_weight=shrink_weight, shrink_momentum=shrink_momentum, shrink_variance=shrink_variance, vector_weight=vector_weight, vector_momentum=vector_momentum, vector_variance=vector_variance)


@jax.custom_vjp
def low(v):
    return lax.optimization_barrier(v.astype(jnp.bfloat16)).astype(jnp.float32)

@jax.custom_vjp
def low_back(v):
    return v

def low_keep(v):
    return (low(v), None)

def low_pass(kept, grad):
    return (grad,)

def back_keep(v):
    return (v, None)

def back_low(kept, grad):
    return (low(grad),)
low.defvjp(low_keep, low_pass)
low_back.defvjp(back_keep, back_low)
highest = lax.Precision.HIGHEST
norm_eps = 1e-05
beta_one = 0.9
beta_two = 0.95
adam_eps = 1e-08
rate_matrix = 0.05
rate_vector = 0.4
decay_matrix = 0.1
masked_score = -1e+30

def layer_norm(values, gain_row, shift_row):
    center = values - lax.optimization_barrier(jnp.mean(values, axis=-1, keepdims=True))
    spread = lax.optimization_barrier(jnp.mean(center * center, axis=-1, keepdims=True))
    return center * lax.rsqrt(spread + norm_eps) * gain_row + shift_row

def segments_of(length_row, total_rows):
    places = jnp.arange(total_rows, dtype=jnp.int32)
    bounds = jnp.cumsum(length_row.astype(jnp.int32)).astype(jnp.int32)
    segment = lax.optimization_barrier(jnp.sum((places[:, None] >= bounds[None, :]).astype(jnp.int32), axis=1)).astype(jnp.int32)
    live_rows = (places < bounds[-1]).astype(jnp.float32)
    return (segment, live_rows)

def attention(queries, keys_all, values_all, segment):
    total_rows = queries.shape[0]
    block_rows = min(512, total_rows)
    scaling = HEAD_DIM ** (-0.5)
    column_index = jnp.arange(total_rows, dtype=jnp.int32)

    def one_block(block_index):
        first_row = (block_index * block_rows).astype(jnp.int32)
        query_part = lax.dynamic_slice_in_dim(queries, first_row, block_rows, 0)
        row_index = first_row + jnp.arange(block_rows, dtype=jnp.int32)
        row_segment = lax.dynamic_slice_in_dim(segment, first_row, block_rows, 0)
        allowed = (row_segment[:, None] == segment[None, :]) & (column_index[None, :] <= row_index[:, None])
        scores = jnp.einsum('qhe,khe->hqk', query_part, keys_all, precision=highest) * scaling
        scores = low_back(scores)
        scores = jnp.where(allowed[None], scores, masked_score)
        highest_score = lax.optimization_barrier(jnp.max(scores, axis=-1, keepdims=True))
        weights = jnp.exp(scores - highest_score)
        probability = low(weights / lax.optimization_barrier(jnp.sum(weights, axis=-1, keepdims=True)))
        return jnp.einsum('hqk,khe->qhe', probability, values_all, precision=highest)
    contexts = lax.map(jax.checkpoint(one_block), jnp.arange(total_rows // block_rows, dtype=jnp.int32))
    return contexts.reshape(queries.shape)

def forward(inputs_row, vector_weight, triple_weight, merge_weight, expand_weight, shrink_weight, segment):
    total_rows = inputs_row.shape[0]
    vectors_low = low(vector_weight)
    triple_low = low(triple_weight)
    merge_low = low(merge_weight)
    expand_low = low(expand_weight)
    shrink_low = low(shrink_weight)
    norm_one = low(layer_norm(inputs_row, vectors_low[0], vectors_low[1]))
    bias_triple = jnp.concatenate([vectors_low[2], jnp.zeros_like(vectors_low[2]), vectors_low[3]])
    mixed = jnp.dot(norm_one, triple_low, precision=highest) + bias_triple
    mixed = low(low_back(mixed)).reshape(total_rows, 3, HEADS, HEAD_DIM)
    context = attention(mixed[:, 0], mixed[:, 1], mixed[:, 2], segment).reshape(total_rows, D)
    context = low(low_back(context))
    branch_one = low_back(jnp.dot(context, merge_low, precision=highest) + vectors_low[4])
    residual = inputs_row + branch_one
    norm_two = low(layer_norm(residual, vectors_low[5], vectors_low[6]))
    expanded = low_back(jnp.dot(norm_two, expand_low, precision=highest) + vectors_low[8:12].reshape(FF))
    activated = low(jax.nn.gelu(expanded, approximate=True))
    branch_two = low_back(jnp.dot(activated, shrink_low, precision=highest) + vectors_low[7])
    return residual + branch_two

def adam_step(weight, momentum, variance, gradient, rate_value, decay_value):
    momentum_new = beta_one * momentum + (1.0 - beta_one) * gradient
    variance_new = beta_two * variance + (1.0 - beta_two) * gradient * gradient
    direction = momentum_new / (1.0 - beta_one ** STEP) / (jnp.sqrt(variance_new / (1.0 - beta_two ** STEP)) + adam_eps)
    return (weight - rate_value * (direction + decay_value * weight), momentum_new, variance_new)

def reference(tokens, cotangent, lengths, triple_weight, triple_momentum, triple_variance, merge_weight, merge_momentum, merge_variance, expand_weight, expand_momentum, expand_variance, shrink_weight, shrink_momentum, shrink_variance, vector_weight, vector_momentum, vector_variance):
    groups = lengths.shape[0]
    token_groups = tokens.astype(jnp.float32).reshape(groups, TOK_DEV, D)
    cotangent_groups = cotangent.astype(jnp.float32).reshape(groups, TOK_DEV, D)
    weights_all = (vector_weight, triple_weight, merge_weight, expand_weight, shrink_weight)

    def advance(running, slices):
        inputs_row, cotangent_row, length_row = slices
        segment, live_rows = segments_of(length_row, TOK_DEV)

        def local_forward(inputs_local, vector_local, triple_local, merge_local, expand_local, shrink_local):
            return forward(inputs_local, vector_local, triple_local, merge_local, expand_local, shrink_local, segment)
        output_row, pullback = jax.vjp(local_forward, inputs_row, *weights_all)
        gradients = pullback(cotangent_row * live_rows[:, None])
        summed = tuple((earlier + addend for earlier, addend in zip(running, gradients[1:])))
        return (summed, (output_row.astype(jnp.bfloat16), gradients[0].astype(jnp.bfloat16)))
    zero_grads = tuple((jnp.zeros_like(array_item) for array_item in weights_all))
    gradient_sums, (outputs_all, input_grads) = lax.scan(advance, zero_grads, (token_groups, cotangent_groups, lengths))
    grad_vector, grad_triple, grad_merge, grad_expand, grad_shrink = gradient_sums
    triple_next, momentum_triple, variance_triple = adam_step(triple_weight, triple_momentum, triple_variance, grad_triple, rate_matrix, decay_matrix)
    merge_next, momentum_merge, variance_merge = adam_step(merge_weight, merge_momentum, merge_variance, grad_merge, rate_matrix, decay_matrix)
    expand_next, momentum_expand, variance_expand = adam_step(expand_weight, expand_momentum, expand_variance, grad_expand, rate_matrix, decay_matrix)
    shrink_next, momentum_shrink, variance_shrink = adam_step(shrink_weight, shrink_momentum, shrink_variance, grad_shrink, rate_matrix, decay_matrix)
    vector_next, momentum_vector, variance_vector = adam_step(vector_weight, vector_momentum, vector_variance, grad_vector, rate_vector, 0.0)
    return (outputs_all.reshape(TOKENS, D), input_grads.reshape(TOKENS, D), triple_next, momentum_triple, variance_triple, merge_next, momentum_merge, variance_merge, expand_next, momentum_expand, variance_expand, shrink_next, momentum_shrink, variance_shrink, vector_next, momentum_vector, variance_vector)
```

```python
import functools

import jax
import jax.numpy as jnp
from jax import lax
from jax.experimental import pallas as pl
from jax.experimental.pallas import tpu as pltpu
from jax.sharding import PartitionSpec as P

HEADS = 17
HEAD_DIM = 64
STEP = 10
MESH = pl.DeviceIdType.MESH


norm_eps = 1e-05
beta_one = 0.9
beta_two = 0.95
adam_eps = 1e-08
rate_matrix = 0.05
rate_vector = 0.4
decay_matrix = 0.1
masked_score = -1e30


def chip_grid(count):
    side = 1
    while 4 * side * side < count:
        side += 1
    return 4, side, side


def row_split(rows, flip):
    tiles = rows // 16
    first = 16 * ((tiles + 1) // 2 if not flip else tiles // 2)
    return ((0, first), (first, rows - first))


def place(sizes):
    _, size_y, size_x = sizes
    core = lax.axis_index("dp")
    chip = lax.axis_index("fsdp")
    return core, lax.div(chip, size_y * size_x), lax.rem(lax.div(chip, size_x), size_y), lax.rem(chip, size_x)


def greet(sizes, core, z, y, x):
    size_z, size_y, size_x = sizes
    barrier = pltpu.get_barrier_semaphore()
    peers = [(1 - core, chip_id(sizes, z, y, x))]
    peers += [(core, chip_id(sizes, lax.rem(z + d, size_z), y, x)) for d in range(1, size_z)]
    peers += [(core, chip_id(sizes, z, lax.rem(y + d, size_y), x)) for d in range(1, size_y)]
    peers += [(core, chip_id(sizes, z, y, lax.rem(x + d, size_x))) for d in range(1, size_x)]
    for peer in peers:
        pl.semaphore_signal(barrier, inc=1, device_id=peer, device_id_type=MESH)
    pl.semaphore_wait(barrier, len(peers))


def chip_id(sizes, z, y, x):
    return (z * sizes[1] + y) * sizes[2] + x


def remote(src, dst, send_sem, recv_sem, peer):
    return pltpu.make_async_remote_copy(
        src_ref=src, dst_ref=dst, send_sem=send_sem, recv_sem=recv_sem,
        device_id=peer, device_id_type=MESH,
    )


def gather_kernel(sizes, splits, *refs):
    arrays = len(splits)
    ins, outs = refs[: arrays + 1], refs[arrays + 1 : 2 * arrays + 2]
    (local_sem, zs_sem, zr_sem, as_sem, ar_sem, bs_sem, br_sem, ps_sem, pr_sem) = refs[2 * arrays + 2 :]
    size_z, side, _ = sizes
    core, z, y, x = place(sizes)
    greet(sizes, core, z, y, x)

    def run(c):
        def at(second, third):
            return (third, second) if c == 0 else (second, third)

        mine = (x, y) if c == 0 else (y, x)
        sends = []

        def back(d2, d3, own=mine):
            return at(lax.rem(own[0] + side - d2, side), lax.rem(own[1] + side - d3, side))

        def peer_of(d2, d3):
            py, px = at(lax.rem(mine[0] + d2, side), lax.rem(mine[1] + d3, side))
            return (core, chip_id(sizes, z, py, px))

        def line(k, yx):
            if k == arrays:
                return outs[k].at[:, yx[0], yx[1]]
            start, rows = splits[k][c]
            return outs[k].at[:, yx[0], yx[1], pl.ds(start, rows), :]

        def go(copy):
            copy.start()
            sends.append(copy)

        def line_copy(k, yx, ss, rs, peer):
            return remote(line(k, yx), line(k, yx), ss, rs, peer)

        def second_copy(k, d2):
            return line_copy(k, (y, x), as_sem.at[k, d2], ar_sem.at[k, d2], peer_of(d2, 0))

        def third_copy(k, d2, d3):
            return line_copy(k, back(d2, 0), bs_sem.at[k, d2, d3], br_sem.at[k, d2, d3], peer_of(0, d3))

        def partner_copy(k, d2, d3):
            return line_copy(
                k, back(d2, d3), ps_sem.at[k, d2, d3], pr_sem.at[k, d2, d3],
                (1 - core, chip_id(sizes, z, y, x)),
            )

        def block(k):
            if k == arrays:
                return ins[k], outs[k].at[z, y, x]
            start, rows = splits[k][c]
            return ins[k].at[pl.ds(start, rows), :], outs[k].at[z, y, x, pl.ds(start, rows), :]

        def z_copy(k, d):
            src, dst = block(k)
            return remote(
                src, dst, zs_sem.at[k, d], zr_sem.at[k, d],
                (core, chip_id(sizes, lax.rem(z + d, size_z), y, x)),
            )

        def own_copy(k):
            src, dst = block(k)
            return pltpu.make_async_copy(src, dst, local_sem.at[k])

        order = [arrays] + list(range(arrays))
        for k in order:
            own_copy(k).start()
            for d in range(1, size_z):
                go(z_copy(k, d))

        def stage_one(k):
            own_copy(k).wait()
            for d in range(1, size_z):
                z_copy(k, d).wait_recv()
            for d in range(1, side):
                go(second_copy(k, d))
            for d in range(1, side):
                go(third_copy(k, 0, d))
            if k < arrays:
                go(partner_copy(k, 0, 0))

        def stage_two(k):
            for d2 in range(1, side):
                second_copy(k, d2).wait_recv()
                for d3 in range(1, side):
                    go(third_copy(k, d2, d3))
                if k < arrays:
                    go(partner_copy(k, d2, 0))

        def stage_three(k):
            for d3 in range(1, side):
                for d2 in range(side):
                    third_copy(k, d2, d3).wait_recv()
                    if k < arrays:
                        go(partner_copy(k, d2, d3))

        stages = (stage_one, stage_two, stage_three)
        for tick in range(len(order) + len(stages) - 1):
            for s in reversed(range(len(stages))):
                if 0 <= tick - s < len(order):
                    stages[s](order[tick - s])

        theirs = (y, x) if c == 0 else (x, y)
        for k in range(arrays):
            start, rows = splits[k][1 - c]
            for d2 in range(side):
                for d3 in range(side):
                    a = lax.rem(theirs[0] + side - d2, side)
                    b = lax.rem(theirs[1] + side - d3, side)
                    yx = (a, b) if c == 0 else (b, a)
                    ref = outs[k].at[:, yx[0], yx[1], pl.ds(start, rows), :]
                    remote(
                        ref, ref, ps_sem.at[k, d2, d3], pr_sem.at[k, d2, d3],
                        (1 - core, chip_id(sizes, z, y, x)),
                    ).wait_recv()
        for copy in sends:
            copy.wait_send()

    pl.when(core == 0)(lambda: run(0))
    pl.when(core == 1)(lambda: run(1))


def gather_all(sizes, shards, vector_shard):
    arrays = len(shards)
    size_z, side, _ = sizes
    splits = tuple(row_split(s.shape[0], k % 2 == 1) for k, s in enumerate(shards))
    everything = tuple(shards) + (vector_shard,)
    dma = pltpu.SemaphoreType.DMA
    return pl.pallas_call(
        functools.partial(gather_kernel, sizes, splits),
        out_shape=[jax.ShapeDtypeStruct(sizes + s.shape, s.dtype) for s in everything],
        in_specs=[pl.BlockSpec(memory_space=pl.ANY)] * (arrays + 1),
        out_specs=[pl.BlockSpec(memory_space=pl.ANY)] * (arrays + 1),
        scratch_shapes=[
            dma((arrays + 1,)),
            dma((arrays + 1, size_z)), dma((arrays + 1, size_z)),
            dma((arrays + 1, side)), dma((arrays + 1, side)),
            dma((arrays + 1, side, side)), dma((arrays + 1, side, side)),
            dma((arrays, side, side)), dma((arrays, side, side)),
        ],
        compiler_params=pltpu.CompilerParams(collective_id=0, has_side_effects=True),
    )(*everything)


def add_into(total, first, extra, blocks):
    counts = list(blocks)
    steps = 1
    for count in counts:
        steps *= count

    def body(step, carry):
        index = []
        for count in reversed(counts):
            index.append(lax.rem(step, count))
            step = lax.div(step, count)
        index = tuple(reversed(index))
        value = first(index)[...].astype(jnp.float32) + extra(index)[...].astype(jnp.float32)
        total(index)[...] = value.astype(total(index).dtype)
        return carry

    lax.fori_loop(0, steps, body, 0)


def scatter_kernel(sizes, splits, *refs):
    arrays = len(splits)
    ins, vec_in = refs[:arrays], refs[arrays]
    outs, vec_out = refs[arrays + 1 : 2 * arrays + 1], refs[2 * arrays + 1]
    (own, part, second, third, fourth, result, vec_slots,
     load_sem, store_sem, as_sem, ar_sem, bs_sem, br_sem, cs_sem, cr_sem, ds_sem, dr_sem,
     es_sem, er_sem, vs_sem, vr_sem, credit) = refs[2 * arrays + 2 :]
    size_z, side, _ = sizes
    core, z, y, x = place(sizes)
    greet(sizes, core, z, y, x)
    partner = (1 - core, chip_id(sizes, z, y, x))

    def run(c):
        sends = []

        def go(copy):
            copy.start()
            sends.append(copy)

        def rows_of(k, which):
            start, rows = splits[k][which]
            return pl.ds(start, rows)

        def height(k, which=c):
            return pl.ds(0, splits[k][which][1])

        def load(k):
            return pltpu.make_async_copy(
                ins[k].at[:, :, :, rows_of(k, c), :], own.at[k, :, :, :, height(k), :], load_sem.at[k]
            )

        def swap(k):
            return remote(
                ins[k].at[:, :, :, rows_of(k, 1 - c), :],
                part.at[k % 2, :, :, :, height(k, 1 - c), :],
                as_sem.at[k], ar_sem.at[k], partner,
            )

        def swapped(k):
            ref = part.at[k % 2, :, :, :, height(k), :]
            return remote(ref, ref, as_sem.at[k], ar_sem.at[k], partner)

        def along(first, d):
            if first == (c == 0):
                other = lax.rem(y + d, side)
                return other, x, (core, chip_id(sizes, z, other, x))
            other = lax.rem(x + d, side)
            return y, other, (core, chip_id(sizes, z, y, other))

        def copy_b(k, d):
            py, px, peer = along(True, d)
            src = own.at[k, :, py, :, height(k), :] if c == 0 else own.at[k, :, :, px, height(k), :]
            return remote(src, second.at[k, d - 1, :, :, height(k), :], bs_sem.at[k, d], br_sem.at[k, d], peer)

        def copy_c(k, d):
            py, px, peer = along(False, d)
            return remote(
                own.at[k, :, py, px, height(k), :], third.at[k, d - 1, :, height(k), :],
                cs_sem.at[k, d], cr_sem.at[k, d], peer,
            )

        def copy_d(k, d):
            pz = lax.rem(z + d, size_z)
            return remote(
                own.at[k, pz, y, x, height(k), :], fourth.at[k, d - 1, height(k), :],
                ds_sem.at[k, d], dr_sem.at[k, d], (core, chip_id(sizes, pz, y, x)),
            )

        def stage_a(k):
            load(k).wait()
            swapped(k).wait_recv()
            h = height(k)
            add_into(
                lambda i: own.at[k, i[0], i[1], i[2], h, :],
                lambda i: own.at[k, i[0], i[1], i[2], h, :],
                lambda i: part.at[k % 2, i[0], i[1], i[2], h, :],
                sizes,
            )
            if k + 2 < arrays:
                pl.semaphore_signal(credit, inc=1, device_id=partner, device_id_type=MESH)
            for d in range(1, side):
                go(copy_b(k, d))
            if k + 2 < arrays:
                pl.semaphore_wait(credit, 1)
                go(swap(k + 2))

        def stage_b(k):
            h = height(k)
            for d in range(1, side):
                copy_b(k, d).wait_recv()

                def mine(i):
                    if c == 0:
                        return own.at[k, i[0], y, i[1], h, :]
                    return own.at[k, i[0], i[1], x, h, :]

                add_into(mine, mine, lambda i: second.at[k, d - 1, i[0], i[1], h, :], (size_z, side))
            for d in range(1, side):
                go(copy_c(k, d))

        def stage_c(k):
            h = height(k)
            for d in range(1, side):
                copy_c(k, d).wait_recv()

                def mine(i):
                    return own.at[k, i[0], y, x, h, :]

                add_into(mine, mine, lambda i: third.at[k, d - 1, i[0], h, :], (size_z,))
            for d in range(1, size_z):
                go(copy_d(k, d))

        def finish(k):
            return remote(
                result.at[k, height(k), :], outs[k].at[rows_of(k, c), :], es_sem.at[k], er_sem.at[k], partner
            )

        def store(k):
            return pltpu.make_async_copy(
                result.at[k, height(k), :], outs[k].at[rows_of(k, c), :], store_sem.at[k]
            )

        def stage_d(k):
            h = height(k)
            total = own[k, z, y, x, h, :].astype(jnp.float32)
            for d in range(1, size_z):
                copy_d(k, d).wait_recv()
                total = total + fourth[k, d - 1, h, :].astype(jnp.float32)
            result[k, h, :] = total
            store(k).start()
            go(finish(k))

        vec_steps = (
            (2, core, lambda i: (i, chip_id(sizes, z, y, x))),
            (side, y, lambda i: (core, chip_id(sizes, z, i, x))),
            (side, x, lambda i: (core, chip_id(sizes, z, y, i))),
            (size_z, z, lambda i: (core, chip_id(sizes, i, y, x))),
        )

        def vec_copy(step, d):
            count, where, peer = vec_steps[step]
            slot = vec_slots.at[step, where]
            return remote(
                slot, slot, vs_sem.at[step, d], vr_sem.at[step, d], peer(lax.rem(where + d, count))
            )

        def vec_arrived(step, d):
            count, where, peer = vec_steps[step]
            source = lax.rem(where + count - d, count)
            slot = vec_slots.at[step, source]
            return remote(slot, slot, vs_sem.at[step, d], vr_sem.at[step, d], peer(lax.rem(where + d, count)))

        def vec_send(step, value):
            count, where, _ = vec_steps[step]
            vec_slots[step, where] = value
            for d in range(1, count):
                go(vec_copy(step, d))

        def vec_sum(step):
            count = vec_steps[step][0]
            for d in range(1, count):
                vec_arrived(step, d).wait_recv()
            total = vec_slots[step, 0]
            for i in range(1, count):
                total = total + vec_slots[step, i]
            return total

        for k in range(arrays):
            load(k).start()
        for k in range(min(2, arrays)):
            go(swap(k))
        vec_send(0, vec_in[...])

        stages = (stage_a, stage_b, stage_c, stage_d)
        for tick in range(arrays + len(stages) - 1):
            for s in reversed(range(len(stages))):
                if 0 <= tick - s < arrays:
                    stages[s](tick - s)
            if tick < 3:
                vec_send(tick + 1, vec_sum(tick))
            elif tick == 3:
                vec_out[...] = vec_sum(3)

        for k in range(arrays):
            store(k).wait()
            start, rows = splits[k][1 - c]
            ref = outs[k].at[pl.ds(start, rows), :]
            remote(ref, ref, es_sem.at[k], er_sem.at[k], partner).wait_recv()
        for copy in sends:
            copy.wait_send()

    pl.when(core == 0)(lambda: run(0))
    pl.when(core == 1)(lambda: run(1))


def scatter_all(sizes, terms, vector_term):
    arrays = len(terms)
    size_z, side, _ = sizes
    rows, width = terms[0].shape[-2:]
    splits = tuple(row_split(rows, k % 2 == 1) for k in range(arrays))
    most = max(part[1] for split in splits for part in split)
    dma = pltpu.SemaphoreType.DMA
    low = jnp.bfloat16
    pair = [dma((arrays,)), dma((arrays,))]
    sides = [dma((arrays, side)), dma((arrays, side))]
    return pl.pallas_call(
        functools.partial(scatter_kernel, sizes, splits),
        out_shape=[jax.ShapeDtypeStruct((rows, width), jnp.float32) for _ in terms]
        + [jax.ShapeDtypeStruct(vector_term.shape, jnp.float32)],
        in_specs=[pl.BlockSpec(memory_space=pl.ANY)] * arrays
        + [pl.BlockSpec(memory_space=pltpu.VMEM)],
        out_specs=[pl.BlockSpec(memory_space=pl.ANY)] * arrays
        + [pl.BlockSpec(memory_space=pltpu.VMEM)],
        scratch_shapes=[
            pltpu.VMEM((arrays,) + sizes + (most, width), low),
            pltpu.VMEM((2,) + sizes + (most, width), low),
            pltpu.VMEM((arrays, side - 1, size_z, side, most, width), low),
            pltpu.VMEM((arrays, side - 1, size_z, most, width), low),
            pltpu.VMEM((arrays, size_z - 1, most, width), low),
            pltpu.VMEM((arrays, most, width), jnp.float32),
            pltpu.VMEM((4, max(size_z, side)) + vector_term.shape, jnp.float32),
            dma((arrays,)), dma((arrays,)),
        ]
        + pair + sides + sides
        + [dma((arrays, size_z)), dma((arrays, size_z))]
        + pair
        + [dma((4, max(size_z, side))), dma((4, max(size_z, side)))]
        + [pltpu.SemaphoreType.REGULAR],
        compiler_params=pltpu.CompilerParams(
            collective_id=1, has_side_effects=True, vmem_limit_bytes=60 * 1024 * 1024
        ),
    )(*terms, vector_term)


def layer_norm(values, gain_row, shift_row):
    center = values - jnp.mean(values, axis=-1, keepdims=True)
    spread = jnp.mean(center * center, axis=-1, keepdims=True)
    return center * lax.rsqrt(spread + norm_eps) * gain_row + shift_row


def gelu_tanh(values):
    return jax.nn.gelu(values, approximate=True)


def segments_of(length_row, total_rows):
    places = jnp.arange(total_rows, dtype=jnp.int32)
    bounds = jnp.cumsum(length_row)
    segment = jnp.sum((places[:, None] >= bounds[None, :]).astype(jnp.int32), axis=1)
    live_rows = (places < bounds[-1]).astype(jnp.float32)
    return (segment, live_rows)


def dot_low(left_side, right_side):
    return jnp.dot(left_side, right_side, preferred_element_type=jnp.float32)


def inner_rows(left_side, right_side):
    return lax.dot_general(
        left_side, right_side, (((0,), (0,)), ((), ())), preferred_element_type=jnp.float32
    )


def times_transposed(left_side, right_side):
    return lax.dot_general(
        left_side, right_side, (((1,), (1,)), ((), ())), preferred_element_type=jnp.float32
    )


def attend_forward(queries, keys_low, values_low, segment):
    total_rows = queries.shape[0]
    places = jnp.arange(total_rows, dtype=jnp.int32)
    allowed = (segment[:, None] == segment[None, :]) & (places[None, :] <= places[:, None])
    scores = jnp.einsum("qhe,khe->hqk", queries, keys_low, preferred_element_type=jnp.float32)
    scores = jnp.where(allowed[None], scores * (HEAD_DIM**-0.5), masked_score)
    weights = jnp.exp(scores - jnp.max(scores, axis=-1, keepdims=True))
    probability = weights / jnp.sum(weights, axis=-1, keepdims=True)
    probs_low = probability.astype(jnp.bfloat16)
    context = jnp.einsum("hqk,khe->qhe", probs_low, values_low, preferred_element_type=jnp.float32)
    return context, probability


def attend_backward(queries, keys_low, values_low, probability, grad_context):
    scaling = HEAD_DIM**-0.5
    probs_low = probability.astype(jnp.bfloat16)
    grad_probs = jnp.einsum(
        "qhe,khe->hqk", grad_context, values_low, preferred_element_type=jnp.float32
    )
    centered = grad_probs - jnp.sum(grad_probs * probability, axis=-1, keepdims=True)
    grad_scores = (probability * centered).astype(jnp.bfloat16)
    grad_query = jnp.einsum("hqk,khe->qhe", grad_scores, keys_low, preferred_element_type=jnp.float32)
    grad_keys = jnp.einsum("hqk,qhe->khe", grad_scores, queries, preferred_element_type=jnp.float32)
    grad_values = jnp.einsum(
        "hqk,qhe->khe", probs_low, grad_context, preferred_element_type=jnp.float32
    )
    return grad_query * scaling, grad_keys * scaling, grad_values


def adam_step(weight, momentum, variance, gradient, rate_value, decay_value):
    momentum_new = beta_one * momentum + (1.0 - beta_one) * gradient
    variance_new = beta_two * variance + (1.0 - beta_two) * gradient * gradient
    direction = (
        momentum_new
        / (1.0 - beta_one**STEP)
        / (jnp.sqrt(variance_new / (1.0 - beta_two**STEP)) + adam_eps)
    )
    return (weight - rate_value * (direction + decay_value * weight), momentum_new, variance_new)


def on_device(
    sizes,
    tokens,
    cotangent,
    lengths,
    triple_weight,
    triple_momentum,
    triple_variance,
    merge_weight,
    merge_momentum,
    merge_variance,
    expand_weight,
    expand_momentum,
    expand_variance,
    shrink_weight,
    shrink_momentum,
    shrink_variance,
    vector_weight,
    vector_momentum,
    vector_variance,
):
    total_rows, width = tokens.shape
    low = jnp.bfloat16
    rows = merge_weight.shape[0]
    count = sizes[0] * sizes[1] * sizes[2]
    blocks = expand_weight.shape[1] // width
    padding = -(blocks * rows) % 16

    def columns(array_item, parts):
        return [array_item[:, i * width : (i + 1) * width] for i in range(parts)]

    def packed(parts):
        whole = jnp.concatenate([p.astype(low) for p in parts], axis=0)
        return jnp.pad(whole, ((0, padding), (0, 0)))

    shards = (
        packed(columns(triple_weight, 3) + [merge_weight]),
        packed(columns(expand_weight, blocks)),
        packed([shrink_weight]),
    )
    all_low = gather_all(sizes, shards, vector_weight.astype(low))

    def unpacked(array_item):
        array_item = array_item.reshape(count, -1, width)
        return [
            array_item[:, i * rows : (i + 1) * rows].reshape(count * rows, width)
            for i in range(blocks)
        ]

    query_low, key_low, value_low, merge_low = unpacked(all_low[0])
    expand_low = unpacked(all_low[1])
    shrink_low = all_low[2].reshape(count, -1, width)[:, : blocks * rows].reshape(-1, width)
    vectors_low = all_low[3].reshape(count, vector_weight.shape[0], rows)
    vectors = vectors_low.transpose(1, 0, 2).reshape(-1, width).astype(jnp.float32)

    segment, live_rows = segments_of(lengths[0], total_rows)
    inputs_float = tokens.astype(jnp.float32)
    norm_one, pull_one = jax.vjp(layer_norm, inputs_float, vectors[0], vectors[1])
    norm_one_low = norm_one.astype(low)
    heads = (total_rows, HEADS, HEAD_DIM)
    queries = (dot_low(norm_one_low, query_low) + vectors[2]).astype(low).reshape(heads)
    keys_low = dot_low(norm_one_low, key_low).astype(low).reshape(heads)
    values_low = (dot_low(norm_one_low, value_low) + vectors[3]).astype(low).reshape(heads)
    context, probability = attend_forward(queries, keys_low, values_low, segment)
    context_low = context.reshape(total_rows, width).astype(low)
    residual = inputs_float + dot_low(context_low, merge_low) + vectors[4]
    norm_two, pull_two = jax.vjp(layer_norm, residual, vectors[5], vectors[6])
    norm_two_low = norm_two.astype(low)
    pulls, activated_low = [], []
    for i in range(blocks):
        activated, pull_gelu = jax.vjp(
            gelu_tanh, dot_low(norm_two_low, expand_low[i]) + vectors[8 + i]
        )
        pulls.append(pull_gelu)
        activated_low.append(activated.astype(low))
    activated_low = jnp.concatenate(activated_low, axis=1)
    layer_output = (residual + dot_low(activated_low, shrink_low) + vectors[7]).astype(low)

    grad_output = cotangent.astype(jnp.float32) * live_rows[:, None]
    grad_output_low = grad_output.astype(low)
    grad_shrink = inner_rows(activated_low, grad_output_low)
    bias_shrink = jnp.sum(grad_output_low, axis=0, dtype=jnp.float32)
    grad_norm_two, grad_expand, bias_expand = 0.0, [], []
    for i in range(blocks):
        grad_active = times_transposed(grad_output_low, shrink_low[i * width : (i + 1) * width])
        grad_expanded_low = pulls[i](grad_active)[0].astype(low)
        grad_expand.append(inner_rows(norm_two_low, grad_expanded_low))
        bias_expand.append(jnp.sum(grad_expanded_low, axis=0, dtype=jnp.float32))
        grad_norm_two = grad_norm_two + times_transposed(grad_expanded_low, expand_low[i])
    grad_residual_norm, gain_two, shift_two = pull_two(grad_norm_two)
    grad_residual = grad_output + grad_residual_norm
    grad_residual_low = grad_residual.astype(low)
    grad_merge = inner_rows(context_low, grad_residual_low)
    bias_merge = jnp.sum(grad_residual_low, axis=0, dtype=jnp.float32)
    grad_context_low = times_transposed(grad_residual_low, merge_low).astype(low).reshape(heads)
    grad_mixed = attend_backward(queries, keys_low, values_low, probability, grad_context_low)
    grad_mixed_low = [g.reshape(total_rows, width).astype(low) for g in grad_mixed]
    grad_triple = [inner_rows(norm_one_low, g) for g in grad_mixed_low]
    bias_query = jnp.sum(grad_mixed_low[0], axis=0, dtype=jnp.float32)
    bias_value = jnp.sum(grad_mixed_low[2], axis=0, dtype=jnp.float32)
    grad_norm_one = (
        times_transposed(grad_mixed_low[0], query_low)
        + times_transposed(grad_mixed_low[1], key_low)
        + times_transposed(grad_mixed_low[2], value_low)
    )
    grad_input_norm, gain_one, shift_one = pull_one(grad_norm_one)
    input_grad = (grad_residual + grad_input_norm).astype(low)
    grad_vector = jnp.stack(
        [gain_one, shift_one, bias_query, bias_value, bias_merge, gain_two, shift_two, bias_shrink]
        + bias_expand
    )

    def spread(parts):
        whole = jnp.concatenate([p.astype(low).reshape(count, -1, width) for p in parts], axis=1)
        whole = jnp.pad(whole, ((0, 0), (0, padding), (0, 0)))
        return whole.reshape(sizes + whole.shape[1:])

    owned_first, owned_expand, owned_shrink, total_vector = scatter_all(
        sizes,
        (spread(grad_triple + [grad_merge]), spread(grad_expand), spread([grad_shrink])),
        grad_vector,
    )

    def beside(array_item, first, parts):
        return jnp.concatenate(
            [array_item[i * rows : (i + 1) * rows] for i in range(first, first + parts)], axis=1
        )

    owned_vector = lax.dynamic_slice_in_dim(total_vector, lax.axis_index("fsdp") * rows, rows, 1)
    triple_part = adam_step(
        triple_weight, triple_momentum, triple_variance, beside(owned_first, 0, 3),
        rate_matrix, decay_matrix,
    )
    merge_part = adam_step(
        merge_weight, merge_momentum, merge_variance, beside(owned_first, 3, 1),
        rate_matrix, decay_matrix,
    )
    expand_part = adam_step(
        expand_weight, expand_momentum, expand_variance, beside(owned_expand, 0, blocks),
        rate_matrix, decay_matrix,
    )
    shrink_part = adam_step(
        shrink_weight, shrink_momentum, shrink_variance, owned_shrink[: blocks * rows],
        rate_matrix, decay_matrix,
    )
    vector_part = adam_step(
        vector_weight, vector_momentum, vector_variance, owned_vector, rate_vector, 0.0
    )
    return (
        (layer_output, input_grad) + triple_part + merge_part + expand_part + shrink_part + vector_part
    )


def solution(mesh):
    token_spec, matrix_spec, vector_spec = P(("dp", "fsdp"), None), P("fsdp", None), P(None, "fsdp")
    return jax.shard_map(
        functools.partial(on_device, chip_grid(mesh.shape["fsdp"])),
        mesh=mesh,
        in_specs=(token_spec,) * 3 + (matrix_spec,) * 12 + (vector_spec,) * 3,
        out_specs=(token_spec,) * 2 + (matrix_spec,) * 12 + (vector_spec,) * 3,
        check_vma=False,
    )
```

```python
import functools

import jax
import jax.numpy as jnp
from jax import lax
from jax.experimental import pallas as pl
from jax.experimental.pallas import tpu as pltpu
from jax.sharding import PartitionSpec as P

HEADS = 17
HEAD_DIM = 64
STEP = 10
MESH = pl.DeviceIdType.MESH


norm_eps = 1e-05
beta_one = 0.9
beta_two = 0.95
adam_eps = 1e-08
rate_matrix = 0.05
rate_vector = 0.4
decay_matrix = 0.1
masked_score = -1e30


def chip_grid(count):
    side = 1
    while 4 * side * side < count:
        side += 1
    return 4, side, side


def row_split(rows, flip):
    tiles = rows // 16
    first = 16 * ((tiles + 1) // 2 if not flip else tiles // 2)
    return ((0, first), (first, rows - first))


def pieces_of(rows, arrays):
    parts = 2 if rows >= 256 else 1
    found = []
    for array in range(arrays):
        spans = row_split(rows, array % 2 == 1)
        for part in range(parts):
            both = []
            for start, height in spans:
                first = height if parts == 1 else 16 * ((height // 16 + 1) // 2)
                both.append((start, first) if part == 0 else (start + first, height - first))
            found.append((array, tuple(both)))
    return tuple(array for array, _ in found), tuple(both for _, both in found)


def place(sizes):
    _, size_y, size_x = sizes
    core = lax.axis_index("dp")
    chip = lax.axis_index("fsdp")
    return core, lax.div(chip, size_y * size_x), lax.rem(lax.div(chip, size_x), size_y), lax.rem(chip, size_x)


def greet(sizes, core, z, y, x):
    size_z, size_y, size_x = sizes
    barrier = pltpu.get_barrier_semaphore()
    peers = [(1 - core, chip_id(sizes, z, y, x))]
    peers += [(core, chip_id(sizes, lax.rem(z + d, size_z), y, x)) for d in range(1, size_z)]
    peers += [(core, chip_id(sizes, z, lax.rem(y + d, size_y), x)) for d in range(1, size_y)]
    peers += [(core, chip_id(sizes, z, y, lax.rem(x + d, size_x))) for d in range(1, size_x)]
    for peer in peers:
        pl.semaphore_signal(barrier, inc=1, device_id=peer, device_id_type=MESH)
    pl.semaphore_wait(barrier, len(peers))


def chip_id(sizes, z, y, x):
    return (z * sizes[1] + y) * sizes[2] + x


def remote(src, dst, send_sem, recv_sem, peer):
    return pltpu.make_async_remote_copy(
        src_ref=src, dst_ref=dst, send_sem=send_sem, recv_sem=recv_sem,
        device_id=peer, device_id_type=MESH,
    )


def gather_kernel(sizes, homes, splits, *refs):
    count = homes[-1] + 1
    arrays = len(splits)
    homes = homes + (count,)
    ins, outs = refs[: count + 1], refs[count + 1 : 2 * count + 2]
    (local_sem, zs_sem, zr_sem, as_sem, ar_sem, bs_sem, br_sem, ps_sem, pr_sem) = refs[2 * count + 2 :]
    size_z, side, _ = sizes
    core, z, y, x = place(sizes)
    greet(sizes, core, z, y, x)

    def run(c):
        def at(second, third):
            return (third, second) if c == 0 else (second, third)

        mine = (x, y) if c == 0 else (y, x)
        sends = []

        def back(d2, d3, own=mine):
            return at(lax.rem(own[0] + side - d2, side), lax.rem(own[1] + side - d3, side))

        def peer_of(d2, d3):
            py, px = at(lax.rem(mine[0] + d2, side), lax.rem(mine[1] + d3, side))
            return (core, chip_id(sizes, z, py, px))

        def line(k, yx):
            if k == arrays:
                return outs[homes[k]].at[:, yx[0], yx[1]]
            start, rows = splits[k][c]
            return outs[homes[k]].at[:, yx[0], yx[1], pl.ds(start, rows), :]

        def go(copy):
            copy.start()
            sends.append(copy)

        def line_copy(k, yx, ss, rs, peer):
            return remote(line(k, yx), line(k, yx), ss, rs, peer)

        def second_copy(k, d2):
            return line_copy(k, (y, x), as_sem.at[k, d2], ar_sem.at[k, d2], peer_of(d2, 0))

        def third_copy(k, d2, d3):
            return line_copy(k, back(d2, 0), bs_sem.at[k, d2, d3], br_sem.at[k, d2, d3], peer_of(0, d3))

        def partner_copy(k, d2, d3):
            return line_copy(
                k, back(d2, d3), ps_sem.at[k, d2, d3], pr_sem.at[k, d2, d3],
                (1 - core, chip_id(sizes, z, y, x)),
            )

        def block(k):
            if k == arrays:
                return ins[homes[k]], outs[homes[k]].at[z, y, x]
            start, rows = splits[k][c]
            return ins[homes[k]].at[pl.ds(start, rows), :], outs[homes[k]].at[z, y, x, pl.ds(start, rows), :]

        def z_copy(k, d):
            src, dst = block(k)
            return remote(
                src, dst, zs_sem.at[k, d], zr_sem.at[k, d],
                (core, chip_id(sizes, lax.rem(z + d, size_z), y, x)),
            )

        def own_copy(k):
            src, dst = block(k)
            return pltpu.make_async_copy(src, dst, local_sem.at[k])

        order = [arrays] + list(range(arrays))

        def begin(k):
            for d in range(1, size_z):
                go(z_copy(k, d))

        for k in order:
            own_copy(k).start()
        for k in order[:3]:
            begin(k)

        def stage_one(k):
            own_copy(k).wait()
            for d in range(1, size_z):
                z_copy(k, d).wait_recv()
            if k < arrays and k + 2 < arrays:
                begin(k + 2)
            for d in range(1, side):
                go(second_copy(k, d))
            for d in range(1, side):
                go(third_copy(k, 0, d))
            if k < arrays:
                go(partner_copy(k, 0, 0))

        def stage_two(k):
            for d2 in range(1, side):
                second_copy(k, d2).wait_recv()
                for d3 in range(1, side):
                    go(third_copy(k, d2, d3))
                if k < arrays:
                    go(partner_copy(k, d2, 0))

        def stage_three(k):
            for d3 in range(1, side):
                for d2 in range(side):
                    third_copy(k, d2, d3).wait_recv()
                    if k < arrays:
                        go(partner_copy(k, d2, d3))

        stages = (stage_one, stage_two, stage_three)
        for tick in range(len(order) + len(stages) - 1):
            for s in reversed(range(len(stages))):
                if 0 <= tick - s < len(order):
                    stages[s](order[tick - s])

        theirs = (y, x) if c == 0 else (x, y)
        for k in range(arrays):
            start, rows = splits[k][1 - c]
            for d2 in range(side):
                for d3 in range(side):
                    a = lax.rem(theirs[0] + side - d2, side)
                    b = lax.rem(theirs[1] + side - d3, side)
                    yx = (a, b) if c == 0 else (b, a)
                    ref = outs[homes[k]].at[:, yx[0], yx[1], pl.ds(start, rows), :]
                    remote(
                        ref, ref, ps_sem.at[k, d2, d3], pr_sem.at[k, d2, d3],
                        (1 - core, chip_id(sizes, z, y, x)),
                    ).wait_recv()
        for copy in sends:
            copy.wait_send()

    pl.when(core == 0)(lambda: run(0))
    pl.when(core == 1)(lambda: run(1))


def gather_all(sizes, shards, vector_shard):
    size_z, side, _ = sizes
    homes, splits = pieces_of(shards[0].shape[0], len(shards))
    arrays = len(splits)
    everything = tuple(shards) + (vector_shard,)
    dma = pltpu.SemaphoreType.DMA
    return pl.pallas_call(
        functools.partial(gather_kernel, sizes, homes, splits),
        out_shape=[jax.ShapeDtypeStruct(sizes + s.shape, s.dtype) for s in everything],
        in_specs=[pl.BlockSpec(memory_space=pl.ANY)] * len(everything),
        out_specs=[pl.BlockSpec(memory_space=pl.ANY)] * len(everything),
        scratch_shapes=[
            dma((arrays + 1,)),
            dma((arrays + 1, size_z)), dma((arrays + 1, size_z)),
            dma((arrays + 1, side)), dma((arrays + 1, side)),
            dma((arrays + 1, side, side)), dma((arrays + 1, side, side)),
            dma((arrays, side, side)), dma((arrays, side, side)),
        ],
        compiler_params=pltpu.CompilerParams(collective_id=0, has_side_effects=True),
    )(*everything)


def add_into(total, first, extra, blocks):
    counts = list(blocks)
    steps = 1
    for count in counts:
        steps *= count

    def body(step, carry):
        index = []
        for count in reversed(counts):
            index.append(lax.rem(step, count))
            step = lax.div(step, count)
        index = tuple(reversed(index))
        value = first(index)[...].astype(jnp.float32) + extra(index)[...].astype(jnp.float32)
        total(index)[...] = value.astype(total(index).dtype)
        return carry

    lax.fori_loop(0, steps, body, 0)


def scatter_kernel(sizes, homes, splits, *refs):
    given = homes[-1] + 1
    arrays = len(splits)
    ins, vec_in = refs[:given], refs[given]
    outs, vec_out = refs[given + 1 : 2 * given + 1], refs[2 * given + 1]
    (own, part, second, third, fourth, result, vec_slots,
     load_sem, store_sem, as_sem, ar_sem, bs_sem, br_sem, cs_sem, cr_sem, ds_sem, dr_sem,
     es_sem, er_sem, vs_sem, vr_sem, credit) = refs[2 * given + 2 :]
    size_z, side, _ = sizes
    core, z, y, x = place(sizes)
    greet(sizes, core, z, y, x)
    partner = (1 - core, chip_id(sizes, z, y, x))

    def run(c):
        sends = []

        def go(copy):
            copy.start()
            sends.append(copy)

        def rows_of(k, which):
            start, rows = splits[k][which]
            return pl.ds(start, rows)

        def height(k, which=c):
            return pl.ds(0, splits[k][which][1])

        def load(k):
            return pltpu.make_async_copy(
                ins[homes[k]].at[:, :, :, rows_of(k, c), :], own.at[k, :, :, :, height(k), :], load_sem.at[k]
            )

        def swap(k):
            return remote(
                ins[homes[k]].at[:, :, :, rows_of(k, 1 - c), :],
                part.at[k % 2, :, :, :, height(k, 1 - c), :],
                as_sem.at[k], ar_sem.at[k], partner,
            )

        def swapped(k):
            ref = part.at[k % 2, :, :, :, height(k), :]
            return remote(ref, ref, as_sem.at[k], ar_sem.at[k], partner)

        def along(first, d):
            if first == (c == 0):
                other = lax.rem(y + d, side)
                return other, x, (core, chip_id(sizes, z, other, x))
            other = lax.rem(x + d, side)
            return y, other, (core, chip_id(sizes, z, y, other))

        def copy_b(k, d):
            py, px, peer = along(True, d)
            src = own.at[k, :, py, :, height(k), :] if c == 0 else own.at[k, :, :, px, height(k), :]
            return remote(src, second.at[k, d - 1, :, :, height(k), :], bs_sem.at[k, d], br_sem.at[k, d], peer)

        def copy_c(k, d):
            py, px, peer = along(False, d)
            return remote(
                own.at[k, :, py, px, height(k), :], third.at[k, d - 1, :, height(k), :],
                cs_sem.at[k, d], cr_sem.at[k, d], peer,
            )

        def copy_d(k, d):
            pz = lax.rem(z + d, size_z)
            return remote(
                own.at[k, pz, y, x, height(k), :], fourth.at[k, d - 1, height(k), :],
                ds_sem.at[k, d], dr_sem.at[k, d], (core, chip_id(sizes, pz, y, x)),
            )

        def stage_a(k):
            load(k).wait()
            swapped(k).wait_recv()
            h = height(k)
            add_into(
                lambda i: own.at[k, i[0], i[1], i[2], h, :],
                lambda i: own.at[k, i[0], i[1], i[2], h, :],
                lambda i: part.at[k % 2, i[0], i[1], i[2], h, :],
                sizes,
            )
            if k + 2 < arrays:
                pl.semaphore_signal(credit, inc=1, device_id=partner, device_id_type=MESH)
            for d in range(1, side):
                go(copy_b(k, d))
            if k + 2 < arrays:
                pl.semaphore_wait(credit, 1)
                go(swap(k + 2))

        def stage_b(k):
            h = height(k)
            for d in range(1, side):
                copy_b(k, d).wait_recv()

                def mine(i):
                    if c == 0:
                        return own.at[k, i[0], y, i[1], h, :]
                    return own.at[k, i[0], i[1], x, h, :]

                add_into(mine, mine, lambda i: second.at[k, d - 1, i[0], i[1], h, :], (size_z, side))
            for d in range(1, side):
                go(copy_c(k, d))

        def stage_c(k):
            h = height(k)
            for d in range(1, side):
                copy_c(k, d).wait_recv()

                def mine(i):
                    return own.at[k, i[0], y, x, h, :]

                add_into(mine, mine, lambda i: third.at[k, d - 1, i[0], h, :], (size_z,))
            for d in range(1, size_z):
                go(copy_d(k, d))

        def finish(k):
            return remote(
                result.at[k, height(k), :], outs[homes[k]].at[rows_of(k, c), :], es_sem.at[k], er_sem.at[k], partner
            )

        def store(k):
            return pltpu.make_async_copy(
                result.at[k, height(k), :], outs[homes[k]].at[rows_of(k, c), :], store_sem.at[k]
            )

        def stage_d(k):
            h = height(k)
            total = own[k, z, y, x, h, :].astype(jnp.float32)
            for d in range(1, size_z):
                copy_d(k, d).wait_recv()
                total = total + fourth[k, d - 1, h, :].astype(jnp.float32)
            result[k, h, :] = total
            store(k).start()
            go(finish(k))

        vec_steps = (
            (2, core, lambda i: (i, chip_id(sizes, z, y, x))),
            (side, y, lambda i: (core, chip_id(sizes, z, i, x))),
            (side, x, lambda i: (core, chip_id(sizes, z, y, i))),
            (size_z, z, lambda i: (core, chip_id(sizes, i, y, x))),
        )

        def vec_copy(step, d):
            count, where, peer = vec_steps[step]
            slot = vec_slots.at[step, where]
            return remote(
                slot, slot, vs_sem.at[step, d], vr_sem.at[step, d], peer(lax.rem(where + d, count))
            )

        def vec_arrived(step, d):
            count, where, peer = vec_steps[step]
            source = lax.rem(where + count - d, count)
            slot = vec_slots.at[step, source]
            return remote(slot, slot, vs_sem.at[step, d], vr_sem.at[step, d], peer(lax.rem(where + d, count)))

        def vec_send(step, value):
            count, where, _ = vec_steps[step]
            vec_slots[step, where] = value
            for d in range(1, count):
                go(vec_copy(step, d))

        def vec_sum(step):
            count = vec_steps[step][0]
            for d in range(1, count):
                vec_arrived(step, d).wait_recv()
            total = vec_slots[step, 0]
            for i in range(1, count):
                total = total + vec_slots[step, i]
            return total

        for k in range(arrays):
            load(k).start()
        for k in range(min(2, arrays)):
            go(swap(k))
        vec_send(0, vec_in[...])

        stages = (stage_a, stage_b, stage_c, stage_d)
        for tick in range(arrays + len(stages) - 1):
            for s in reversed(range(len(stages))):
                if 0 <= tick - s < arrays:
                    stages[s](tick - s)
            if tick < 3:
                vec_send(tick + 1, vec_sum(tick))
            elif tick == 3:
                vec_out[...] = vec_sum(3)

        for k in range(arrays):
            store(k).wait()
            start, rows = splits[k][1 - c]
            ref = outs[homes[k]].at[pl.ds(start, rows), :]
            remote(ref, ref, es_sem.at[k], er_sem.at[k], partner).wait_recv()
        for copy in sends:
            copy.wait_send()

    pl.when(core == 0)(lambda: run(0))
    pl.when(core == 1)(lambda: run(1))


def scatter_all(sizes, terms, vector_term):
    size_z, side, _ = sizes
    rows, width = terms[0].shape[-2:]
    homes, splits = pieces_of(rows, len(terms))
    arrays = len(splits)
    most = max(part[1] for split in splits for part in split)
    dma = pltpu.SemaphoreType.DMA
    low = jnp.bfloat16
    pair = [dma((arrays,)), dma((arrays,))]
    sides = [dma((arrays, side)), dma((arrays, side))]
    return pl.pallas_call(
        functools.partial(scatter_kernel, sizes, homes, splits),
        out_shape=[jax.ShapeDtypeStruct((rows, width), jnp.float32) for _ in terms]
        + [jax.ShapeDtypeStruct(vector_term.shape, jnp.float32)],
        in_specs=[pl.BlockSpec(memory_space=pl.ANY)] * len(terms)
        + [pl.BlockSpec(memory_space=pltpu.VMEM)],
        out_specs=[pl.BlockSpec(memory_space=pl.ANY)] * len(terms)
        + [pl.BlockSpec(memory_space=pltpu.VMEM)],
        scratch_shapes=[
            pltpu.VMEM((arrays,) + sizes + (most, width), low),
            pltpu.VMEM((2,) + sizes + (most, width), low),
            pltpu.VMEM((arrays, side - 1, size_z, side, most, width), low),
            pltpu.VMEM((arrays, side - 1, size_z, most, width), low),
            pltpu.VMEM((arrays, size_z - 1, most, width), low),
            pltpu.VMEM((arrays, most, width), jnp.float32),
            pltpu.VMEM((4, max(size_z, side)) + vector_term.shape, jnp.float32),
            dma((arrays,)), dma((arrays,)),
        ]
        + pair + sides + sides
        + [dma((arrays, size_z)), dma((arrays, size_z))]
        + pair
        + [dma((4, max(size_z, side))), dma((4, max(size_z, side)))]
        + [pltpu.SemaphoreType.REGULAR],
        compiler_params=pltpu.CompilerParams(
            collective_id=1, has_side_effects=True, vmem_limit_bytes=60 * 1024 * 1024
        ),
    )(*terms, vector_term)


def layer_norm(values, gain_row, shift_row):
    center = values - jnp.mean(values, axis=-1, keepdims=True)
    spread = jnp.mean(center * center, axis=-1, keepdims=True)
    return center * lax.rsqrt(spread + norm_eps) * gain_row + shift_row


def gelu_tanh(values):
    return jax.nn.gelu(values, approximate=True)


def segments_of(length_row, total_rows):
    places = jnp.arange(total_rows, dtype=jnp.int32)
    bounds = jnp.cumsum(length_row)
    segment = jnp.sum((places[:, None] >= bounds[None, :]).astype(jnp.int32), axis=1)
    live_rows = (places < bounds[-1]).astype(jnp.float32)
    return (segment, live_rows)


def dot_low(left_side, right_side):
    return jnp.dot(left_side, right_side, preferred_element_type=jnp.float32)


def inner_rows(left_side, right_side):
    return lax.dot_general(
        left_side, right_side, (((0,), (0,)), ((), ())), preferred_element_type=jnp.float32
    )


def times_transposed(left_side, right_side):
    return lax.dot_general(
        left_side, right_side, (((1,), (1,)), ((), ())), preferred_element_type=jnp.float32
    )


def attend_forward(queries, keys_low, values_low, segment):
    total_rows = queries.shape[0]
    places = jnp.arange(total_rows, dtype=jnp.int32)
    allowed = (segment[:, None] == segment[None, :]) & (places[None, :] <= places[:, None])
    scores = jnp.einsum("qhe,khe->hqk", queries, keys_low, preferred_element_type=jnp.float32)
    scores = jnp.where(allowed[None], scores * (HEAD_DIM**-0.5), masked_score)
    weights = jnp.exp(scores - jnp.max(scores, axis=-1, keepdims=True))
    probability = weights / jnp.sum(weights, axis=-1, keepdims=True)
    probs_low = probability.astype(jnp.bfloat16)
    context = jnp.einsum("hqk,khe->qhe", probs_low, values_low, preferred_element_type=jnp.float32)
    return context, probability


def attend_backward(queries, keys_low, values_low, probability, grad_context):
    scaling = HEAD_DIM**-0.5
    probs_low = probability.astype(jnp.bfloat16)
    grad_probs = jnp.einsum(
        "qhe,khe->hqk", grad_context, values_low, preferred_element_type=jnp.float32
    )
    centered = grad_probs - jnp.sum(grad_probs * probability, axis=-1, keepdims=True)
    grad_scores = (probability * centered).astype(jnp.bfloat16)
    grad_query = jnp.einsum("hqk,khe->qhe", grad_scores, keys_low, preferred_element_type=jnp.float32)
    grad_keys = jnp.einsum("hqk,qhe->khe", grad_scores, queries, preferred_element_type=jnp.float32)
    grad_values = jnp.einsum(
        "hqk,qhe->khe", probs_low, grad_context, preferred_element_type=jnp.float32
    )
    return grad_query * scaling, grad_keys * scaling, grad_values


def adam_step(weight, momentum, variance, gradient, rate_value, decay_value):
    momentum_new = beta_one * momentum + (1.0 - beta_one) * gradient
    variance_new = beta_two * variance + (1.0 - beta_two) * gradient * gradient
    direction = (
        momentum_new
        / (1.0 - beta_one**STEP)
        / (jnp.sqrt(variance_new / (1.0 - beta_two**STEP)) + adam_eps)
    )
    return (weight - rate_value * (direction + decay_value * weight), momentum_new, variance_new)


def on_device(
    sizes,
    tokens,
    cotangent,
    lengths,
    triple_weight,
    triple_momentum,
    triple_variance,
    merge_weight,
    merge_momentum,
    merge_variance,
    expand_weight,
    expand_momentum,
    expand_variance,
    shrink_weight,
    shrink_momentum,
    shrink_variance,
    vector_weight,
    vector_momentum,
    vector_variance,
):
    total_rows, width = tokens.shape
    low = jnp.bfloat16
    rows = merge_weight.shape[0]
    count = sizes[0] * sizes[1] * sizes[2]
    blocks = expand_weight.shape[1] // width
    padding = -(blocks * rows) % 16

    def columns(array_item, parts):
        return [array_item[:, i * width : (i + 1) * width] for i in range(parts)]

    def packed(parts):
        whole = jnp.concatenate([p.astype(low) for p in parts], axis=0)
        return jnp.pad(whole, ((0, padding), (0, 0)))

    shards = (
        packed(columns(triple_weight, 3) + [merge_weight]),
        packed(columns(expand_weight, blocks)),
        packed([shrink_weight]),
    )
    all_low = gather_all(sizes, shards, vector_weight.astype(low))

    def unpacked(array_item):
        array_item = array_item.reshape(count, -1, width)
        return [
            array_item[:, i * rows : (i + 1) * rows].reshape(count * rows, width)
            for i in range(blocks)
        ]

    query_low, key_low, value_low, merge_low = unpacked(all_low[0])
    expand_low = unpacked(all_low[1])
    shrink_low = all_low[2].reshape(count, -1, width)[:, : blocks * rows].reshape(-1, width)
    vectors_low = all_low[3].reshape(count, vector_weight.shape[0], rows)
    vectors = vectors_low.transpose(1, 0, 2).reshape(-1, width).astype(jnp.float32)

    segment, live_rows = segments_of(lengths[0], total_rows)
    inputs_float = tokens.astype(jnp.float32)
    norm_one, pull_one = jax.vjp(layer_norm, inputs_float, vectors[0], vectors[1])
    norm_one_low = norm_one.astype(low)
    heads = (total_rows, HEADS, HEAD_DIM)
    queries = (dot_low(norm_one_low, query_low) + vectors[2]).astype(low).reshape(heads)
    keys_low = dot_low(norm_one_low, key_low).astype(low).reshape(heads)
    values_low = (dot_low(norm_one_low, value_low) + vectors[3]).astype(low).reshape(heads)
    context, probability = attend_forward(queries, keys_low, values_low, segment)
    context_low = context.reshape(total_rows, width).astype(low)
    residual = inputs_float + dot_low(context_low, merge_low) + vectors[4]
    norm_two, pull_two = jax.vjp(layer_norm, residual, vectors[5], vectors[6])
    norm_two_low = norm_two.astype(low)
    pulls, activated_low = [], []
    for i in range(blocks):
        activated, pull_gelu = jax.vjp(
            gelu_tanh, dot_low(norm_two_low, expand_low[i]) + vectors[8 + i]
        )
        pulls.append(pull_gelu)
        activated_low.append(activated.astype(low))
    activated_low = jnp.concatenate(activated_low, axis=1)
    layer_output = (residual + dot_low(activated_low, shrink_low) + vectors[7]).astype(low)

    grad_output = cotangent.astype(jnp.float32) * live_rows[:, None]
    grad_output_low = grad_output.astype(low)
    grad_shrink = inner_rows(activated_low, grad_output_low)
    bias_shrink = jnp.sum(grad_output_low, axis=0, dtype=jnp.float32)
    grad_norm_two, grad_expand, bias_expand = 0.0, [], []
    for i in range(blocks):
        grad_active = times_transposed(grad_output_low, shrink_low[i * width : (i + 1) * width])
        grad_expanded_low = pulls[i](grad_active)[0].astype(low)
        grad_expand.append(inner_rows(norm_two_low, grad_expanded_low))
        bias_expand.append(jnp.sum(grad_expanded_low, axis=0, dtype=jnp.float32))
        grad_norm_two = grad_norm_two + times_transposed(grad_expanded_low, expand_low[i])
    grad_residual_norm, gain_two, shift_two = pull_two(grad_norm_two)
    grad_residual = grad_output + grad_residual_norm
    grad_residual_low = grad_residual.astype(low)
    grad_merge = inner_rows(context_low, grad_residual_low)
    bias_merge = jnp.sum(grad_residual_low, axis=0, dtype=jnp.float32)
    grad_context_low = times_transposed(grad_residual_low, merge_low).astype(low).reshape(heads)
    grad_mixed = attend_backward(queries, keys_low, values_low, probability, grad_context_low)
    grad_mixed_low = [g.reshape(total_rows, width).astype(low) for g in grad_mixed]
    grad_triple = [inner_rows(norm_one_low, g) for g in grad_mixed_low]
    bias_query = jnp.sum(grad_mixed_low[0], axis=0, dtype=jnp.float32)
    bias_value = jnp.sum(grad_mixed_low[2], axis=0, dtype=jnp.float32)
    grad_norm_one = (
        times_transposed(grad_mixed_low[0], query_low)
        + times_transposed(grad_mixed_low[1], key_low)
        + times_transposed(grad_mixed_low[2], value_low)
    )
    grad_input_norm, gain_one, shift_one = pull_one(grad_norm_one)
    input_grad = (grad_residual + grad_input_norm).astype(low)
    grad_vector = jnp.stack(
        [gain_one, shift_one, bias_query, bias_value, bias_merge, gain_two, shift_two, bias_shrink]
        + bias_expand
    )

    def spread(parts):
        whole = jnp.concatenate([p.astype(low).reshape(count, -1, width) for p in parts], axis=1)
        whole = jnp.pad(whole, ((0, 0), (0, padding), (0, 0)))
        return whole.reshape(sizes + whole.shape[1:])

    owned_first, owned_expand, owned_shrink, total_vector = scatter_all(
        sizes,
        (spread(grad_triple + [grad_merge]), spread(grad_expand), spread([grad_shrink])),
        grad_vector,
    )

    def beside(array_item, first, parts):
        return jnp.concatenate(
            [array_item[i * rows : (i + 1) * rows] for i in range(first, first + parts)], axis=1
        )

    owned_vector = lax.dynamic_slice_in_dim(total_vector, lax.axis_index("fsdp") * rows, rows, 1)
    triple_part = adam_step(
        triple_weight, triple_momentum, triple_variance, beside(owned_first, 0, 3),
        rate_matrix, decay_matrix,
    )
    merge_part = adam_step(
        merge_weight, merge_momentum, merge_variance, beside(owned_first, 3, 1),
        rate_matrix, decay_matrix,
    )
    expand_part = adam_step(
        expand_weight, expand_momentum, expand_variance, beside(owned_expand, 0, blocks),
        rate_matrix, decay_matrix,
    )
    shrink_part = adam_step(
        shrink_weight, shrink_momentum, shrink_variance, owned_shrink[: blocks * rows],
        rate_matrix, decay_matrix,
    )
    vector_part = adam_step(
        vector_weight, vector_momentum, vector_variance, owned_vector, rate_vector, 0.0
    )
    return (
        (layer_output, input_grad) + triple_part + merge_part + expand_part + shrink_part + vector_part
    )


def solution(mesh):
    token_spec, matrix_spec, vector_spec = P(("dp", "fsdp"), None), P("fsdp", None), P(None, "fsdp")
    return jax.shard_map(
        functools.partial(on_device, chip_grid(mesh.shape["fsdp"])),
        mesh=mesh,
        in_specs=(token_spec,) * 3 + (matrix_spec,) * 12 + (vector_spec,) * 3,
        out_specs=(token_spec,) * 2 + (matrix_spec,) * 12 + (vector_spec,) * 3,
        check_vma=False,
    )
```
